256 devices in a mesh: rep: 4 (over z_hi), dp: 16 (over z_lo, y, core), fsdp: 4 (over x).
Axes of the slice: x: 4, y: 4, z: 8 (z_hi: 4, z_lo: 2; z = z_hi * 2 + z_lo), core: 2. Of those that a mesh axis runs over, the one named last changes fastest.
Arguments:
- projections: bfloat16 [576, 128, 16, 384], P(('rep', 'dp'), None, 'fsdp'), may hold values from -150 to 150
- cotangent: bfloat16 [576, 128, 3200], P(('rep', 'dp'), 'fsdp'), may hold values from -24 to 24
- out_weight: bfloat16 [16, 128, 3200], P('fsdp'), may hold values from -0.125 to 0.125
- tile_counts: int32 [4, 16], P('rep'), may hold values from 1 to 9, as said below
- fragment: int32 [1], replicated, may hold values from 0 to 4
- drift: float32 [4, 16, 128, 3200], P('rep', 'fsdp', 'dp'), may hold values from -6 to 6
Outputs:
- gradients: bfloat16 [576, 128, 16, 384], P(('rep', 'dp'), None, 'fsdp')
- weight_grad: float32 [4, 16, 128, 3200], P('rep', 'fsdp', 'dp')
- synced: float32 [16, 128, 640], P('fsdp', 'dp')
The draws below stay inside these ranges and needn't reach their ends.
Inputs may be any that keep to these rules, and one draw needn't show every extreme that they name: `tile_counts`: the live tiles of one replica's images total exactly 96, and in every replica some image has 9 of them.
All inputs are finite; a program needn't handle non-finite values.
Results may differ from the reference program's by a relative error of at most 0.022.
Values may be sent and summed in bfloat16 or wider, within the bound.
No kernel may reach another device: no remote copies, remote signals or barrier semaphores. Data moves between devices by JAX's collectives and lax.ppermute only.
A program may use at most 128 MiB of HBM per device.

```python
import jax
import jax.numpy as jnp
from jax import lax

D = 3200
HEADS = 16
HD = 128
PATCHES = 128
CAP = 6
FRAGS = 5
HOME = 9
IMAGES = 16
REPLICAS = 4
TILES = 576
FRAG_W = 640


def draw_projections(key, part):
    key = jax.random.fold_in(key, 11)
    shape = (TILES, PATCHES, HEADS, 3 * HD)
    entries = jnp.clip(jax.random.normal(key, shape, jnp.float32), -4.0, 4.0)
    return entries.astype(jnp.bfloat16)


def draw_tile_counts(key, part):
    key = jax.random.fold_in(key, 23)
    spare = HOME - 1
    others = (IMAGES - 1) * spare
    wanted = (CAP - 1) * IMAGES - spare

    def one_replica(row_key):
        keys = jax.random.split(row_key, 2)
        order = jax.random.permutation(keys[0], others)
        chosen = (order < wanted).astype(jnp.int32).reshape(IMAGES - 1, spare).sum(axis=1)
        extras = jnp.concatenate([jnp.full((1,), spare, jnp.int32), chosen])
        return 1 + jax.random.permutation(keys[1], extras)
    return jax.vmap(one_replica)(jax.random.split(key, REPLICAS)).astype(jnp.int32)


def levels(own_key, shape, pieces, smallest, largest):
    def one(dim, shards_of):
        steps = jax.random.uniform(jax.random.fold_in(jax.random.fold_in(own_key, 6), dim), (shards_of,), jnp.float32, smallest / len(pieces), largest / len(pieces))
        return jnp.repeat(jnp.exp(steps), shape[dim] // shards_of).reshape((-1,) + (1,) * (len(shape) - dim - 1))

    level = one(*pieces[0])
    for cut in pieces[1:]:
        level = level * one(*cut)
    return level


def centred(key, dims, width, limit, shards=(), kind=jnp.bfloat16):
    factor_of = levels(key, dims, shards, -0.22, 0.18) if shards else 1.0
    values = jax.random.normal(key, dims, jnp.float32) * width * factor_of
    return jnp.minimum(jnp.maximum(values, -limit), limit).astype(kind)


def setup_inputs(seed: int = 0) -> dict:
    streams_of = jax.random.split(jax.random.key(seed), 7)
    projections = draw_projections(jax.random.fold_in(streams_of[6], 71), 0)
    cotangent = centred(streams_of[1], (TILES, PATCHES, D), 4.0, 24.0, ((0, 64), (1, 4)))
    out_weight = centred(streams_of[2], (HEADS, HD, D), (HEADS * HD) ** -0.5, 0.125, ((0, 4),))
    tile_counts = draw_tile_counts(jax.random.fold_in(streams_of[6], 71), 0)
    fragment = jax.random.randint(streams_of[4], (1,), 0, FRAGS).astype(jnp.int32)
    drift = centred(streams_of[5], (REPLICAS, HEADS, HD, D), 1.0, 6.0, ((0, 4), (1, 4), (2, 16)), jnp.float32)
    return dict(projections=projections, cotangent=cotangent, out_weight=out_weight, tile_counts=tile_counts, fragment=fragment, drift=drift)


def tile_grads(tile_proj, dy_tile, weight):
    tile_data = tile_proj.astype(jnp.float32)
    queries = tile_data[:, :, 0:HD]
    key_rows = tile_data[:, :, HD:2 * HD]
    value_rows = tile_data[:, :, 2 * HD:3 * HD]
    factor = HD ** -0.5
    scores = jnp.einsum("ihe,jhe->hij", queries, key_rows) * factor
    prob_values = jax.nn.softmax(scores, axis=-1)
    probs_wide = lax.optimization_barrier(prob_values.astype(jnp.bfloat16)).astype(jnp.float32)
    context = jnp.einsum("hij,jhe->ihe", probs_wide, value_rows).astype(jnp.bfloat16)
    dy_wide = dy_tile.astype(jnp.float32)
    context_grad = jnp.einsum("id,hed->ihe", dy_wide, weight).astype(jnp.bfloat16)
    grad_wide = lax.optimization_barrier(context_grad).astype(jnp.float32)
    value_grad = jnp.einsum("hij,ihe->jhe", probs_wide, grad_wide).astype(jnp.bfloat16)
    prob_grad = jnp.einsum("ihe,jhe->hij", grad_wide, value_rows)
    centre = jnp.sum(prob_values * prob_grad, axis=-1, keepdims=True)
    score_grad = (prob_values * (prob_grad - centre) * factor).astype(jnp.bfloat16)
    score_wide = lax.optimization_barrier(score_grad).astype(jnp.float32)
    query_grad = jnp.einsum("hij,jhe->ihe", score_wide, key_rows).astype(jnp.bfloat16)
    key_grad = jnp.einsum("hij,ihe->jhe", score_wide, queries).astype(jnp.bfloat16)
    return jnp.concatenate([query_grad, key_grad, value_grad], axis=-1), context


def reference(projections, cotangent, out_weight, tile_counts, fragment, drift):
    weight = out_weight.astype(jnp.float32)
    per_replica = IMAGES * HOME
    grad_parts = []
    weight_parts = []
    for replica in range(REPLICAS):
        def tile_step(running, slot_index):
            row_index = (replica * per_replica + slot_index).astype(jnp.int32)
            tile_proj = lax.dynamic_index_in_dim(projections, row_index, 0, keepdims=False)
            dy_tile = lax.dynamic_index_in_dim(cotangent, row_index, 0, keepdims=False)
            image_count = tile_counts[replica, slot_index // HOME]
            is_live = slot_index % HOME < image_count
            tile_out, context = tile_grads(tile_proj, dy_tile, weight)
            tile_out = jnp.where(is_live, tile_out, jnp.zeros_like(tile_out))
            context_wide = jnp.where(is_live, context.astype(jnp.float32), jnp.zeros(context.shape, jnp.float32))
            running = running + jnp.einsum("ihe,id->hed", context_wide, dy_tile.astype(jnp.float32))
            return running, tile_out

        start_sum = jnp.zeros((HEADS, HD, D), jnp.float32)
        running, tile_outs = lax.scan(tile_step, start_sum, jnp.arange(per_replica, dtype=jnp.int32))
        grad_parts.append(tile_outs)
        weight_parts.append(running / (CAP * IMAGES))
    gradients = jnp.concatenate(grad_parts, axis=0)
    weight_grad = jnp.stack(weight_parts, axis=0)
    fragment_cols = lax.dynamic_slice_in_dim(drift, (fragment[0] * FRAG_W).astype(jnp.int32), FRAG_W, 3)
    synced = jnp.sum(fragment_cols, axis=0) / REPLICAS
    return gradients, weight_grad, synced
```

```python
import functools

import jax
import jax.numpy as jnp
from jax import lax
from jax.experimental import pallas as pl
from jax.experimental.pallas import tpu as pltpu
from jax.sharding import PartitionSpec as P

CAP = 6
FRAGS = 5
LANES = 128
VMEM_LIMIT = 40 * 1024 * 1024
F32 = jnp.float32
BF16 = jnp.bfloat16

NT = (((1,), (1,)), ((), ()))
TN = (((0,), (0,)), ((), ()))


def vmem():
    return pl.BlockSpec(memory_space=pltpu.VMEM)


def params(**extra):
    return pltpu.CompilerParams(vmem_limit_bytes=VMEM_LIMIT, **extra)


def forward_kernel(scal, proj, qkv_out, probs_out, ctx_out, wide):
    heads, tokens, three = qkv_out.shape[1:]
    hd = three // 3
    factor = hd ** (-0.5)
    live = pl.program_id(0) < scal[0]
    qkv = jnp.swapaxes(proj[0], 0, 1)
    qkv_out[0] = qkv
    for h in range(heads):
        q = qkv[h, :, 0:hd]
        k = qkv[h, :, hd : 2 * hd]
        v = qkv[h, :, 2 * hd : 3 * hd]
        scores = lax.dot_general(q, k, NT, preferred_element_type=F32) * factor
        shifted = jnp.exp(scores - jnp.max(scores, axis=-1, keepdims=True))
        probs = shifted / jnp.sum(shifted, axis=-1, keepdims=True)
        probs_out[0, h] = probs
        context = jnp.dot(probs.astype(BF16), v, preferred_element_type=F32)
        context = jnp.where(live, context, 0.0)
        wide[h] = context.T
    slots = scal.shape[0] - 2
    for j in range(slots):
        row = pl.multiple_of(scal[2 + j] * 8, 8)
        rows = jnp.concatenate([wide[h, pl.ds(row, 8), :] for h in range(heads)], axis=0)
        ctx_out[j * 8 * heads : (j + 1) * 8 * heads, :] = rows.astype(BF16)


def forward(scal, projections):
    tiles, tokens, heads, three = projections.shape
    hd = three // 3
    return pl.pallas_call(
        forward_kernel,
        grid_spec=pltpu.PrefetchScalarGridSpec(
            num_scalar_prefetch=1,
            grid=(tiles,),
            in_specs=[pl.BlockSpec((1, tokens, heads, three), lambda t, s: (t, 0, 0, 0))],
            out_specs=[
                pl.BlockSpec((1, heads, tokens, three), lambda t, s: (t, 0, 0, 0)),
                pl.BlockSpec((1, heads, tokens, tokens), lambda t, s: (t, 0, 0, 0)),
                pl.BlockSpec((heads * hd, tokens), lambda t, s: (0, t)),
            ],
            scratch_shapes=[pltpu.VMEM((heads, hd, tokens), F32)],
        ),
        out_shape=[
            jax.ShapeDtypeStruct((tiles, heads, tokens, three), BF16),
            jax.ShapeDtypeStruct((tiles, heads, tokens, tokens), F32),
            jax.ShapeDtypeStruct((heads * hd, tiles * tokens), BF16),
        ],
        compiler_params=params(),
        cost_estimate=pl.CostEstimate(
            flops=4 * tiles * heads * tokens * tokens * hd * 4, bytes_accessed=12_000_000, transcendentals=0
        ),
        name="forward",
    )(scal, projections)


def place(scal, pieces, gathered):
    me = scal[1]
    for step, piece in enumerate(pieces):
        block = lax.rem(me + step, 4)
        gathered[:, pl.ds(block, 1)] = piece[...][:, None]


def chunk_kernel(first, with_ctx_grad, start, scal, own, plus1, plus2, minus1, ctx, weight, *rest):
    if with_ctx_grad:
        if first:
            keep, send, acc_out, gathered, w_part, sem = rest
        else:
            acc_in, keep, send, acc_out, gathered, w_part, sem = rest
    else:
        keep, send, gathered = rest
    tiles, _, tokens, cols = gathered.shape
    if with_ctx_grad:
        copy = pltpu.make_async_copy(weight.at[:, start : start + cols], w_part, sem)
        copy.start()
    place(scal, (own, plus1, plus2, minus1), gathered)
    cot = gathered[...].reshape(tiles * 4 * tokens, cols)
    half = keep.shape[0] * keep.shape[1]
    sums = jnp.dot(ctx[...], cot, preferred_element_type=F32)
    keep[...] = sums[:half].astype(BF16).reshape(keep.shape)
    send[...] = sums[half:].astype(BF16).reshape(send.shape)
    if with_ctx_grad:
        copy.wait()
        grad = lax.dot_general(cot, w_part[...], NT, preferred_element_type=F32)
        acc_out[...] = grad if first else acc_in[...] + grad


def chunk(scal, pieces, ctx, weight, acc, start, first, with_ctx_grad):
    tiles, tokens, cols = pieces[0].shape
    rows, depth = ctx.shape
    out_shape = [jax.ShapeDtypeStruct((8, rows // 16, cols), BF16)] * 2
    scratch = [pltpu.VMEM((tiles, 4, tokens, cols), BF16)]
    operands = [scal, *pieces, ctx, weight]
    specs = [pl.BlockSpec(memory_space=pltpu.SMEM)] + [vmem()] * 5 + [pl.BlockSpec(memory_space=pl.ANY)]
    aliases = {}
    if with_ctx_grad:
        out_shape.append(jax.ShapeDtypeStruct((depth, rows), F32))
        scratch += [pltpu.VMEM((rows, cols), BF16), pltpu.SemaphoreType.DMA]
        if not first:
            operands.append(acc)
            specs.append(vmem())
            aliases = {len(operands) - 1: 2}
    return pl.pallas_call(
        functools.partial(chunk_kernel, first, with_ctx_grad, start),
        in_specs=specs,
        out_specs=[vmem()] * len(out_shape),
        out_shape=out_shape,
        scratch_shapes=scratch,
        input_output_aliases=aliases,
        compiler_params=params(),
        cost_estimate=pl.CostEstimate(
            flops=(4 if with_ctx_grad else 2) * rows * depth * cols, bytes_accessed=8_000_000, transcendentals=0
        ),
        name="chunk",
    )(*operands)


def backward_kernel(start, scal, own, plus1, plus2, minus1, acc, qkv, probs_in, weight, out, gathered, w_part, grads, sem):
    heads, tokens, three = qkv.shape[1:]
    hd = three // 3
    factor = hd ** (-0.5)
    cols = w_part.shape[1]
    tile = pl.program_id(0)

    @pl.when(tile == 0)
    def _():
        copy = pltpu.make_async_copy(weight.at[:, start : start + cols], w_part, sem)
        copy.start()
        copy.wait()

    @pl.when(tile < scal[0])
    def _():
        place(scal, (own, plus1, plus2, minus1), gathered)
        cot = gathered[0].reshape(tokens, cols)
        ctx_grad = acc[...] + lax.dot_general(cot, w_part[...], NT, preferred_element_type=F32)
        ctx_grad = ctx_grad.astype(BF16)
        for h in range(heads):
            q = qkv[0, h, :, 0:hd]
            k = qkv[0, h, :, hd : 2 * hd]
            v = qkv[0, h, :, 2 * hd : 3 * hd]
            dctx = ctx_grad[:, h * hd : (h + 1) * hd]
            probs = probs_in[0, h]
            prob_grad = lax.dot_general(dctx, v, NT, preferred_element_type=F32)
            value_grad = lax.dot_general(probs.astype(BF16), dctx, TN, preferred_element_type=F32)
            centre = jnp.sum(probs * prob_grad, axis=-1, keepdims=True)
            score_grad = (probs * (prob_grad - centre) * factor).astype(BF16)
            query_grad = jnp.dot(score_grad, k, preferred_element_type=F32)
            key_grad = lax.dot_general(score_grad, q, TN, preferred_element_type=F32)
            grads[h, :, 0:hd] = query_grad.astype(BF16)
            grads[h, :, hd : 2 * hd] = key_grad.astype(BF16)
            grads[h, :, 2 * hd : 3 * hd] = value_grad.astype(BF16)
        out[0] = jnp.swapaxes(grads[...], 0, 1)

    @pl.when(tile >= scal[0])
    def _():
        out[...] = jnp.zeros_like(out)


def backward(scal, pieces, acc, qkv, probs, weight, start):
    tiles, block, cols = pieces[0].shape
    heads, tokens, three = qkv.shape[1:]
    rows = weight.shape[0]
    piece_spec = pl.BlockSpec((1, block, cols), lambda t, s: (t, 0, 0))
    return pl.pallas_call(
        functools.partial(backward_kernel, start),
        grid_spec=pltpu.PrefetchScalarGridSpec(
            num_scalar_prefetch=1,
            grid=(tiles,),
            in_specs=[piece_spec] * 4
            + [
                pl.BlockSpec((tokens, rows), lambda t, s: (t, 0)),
                pl.BlockSpec((1, heads, tokens, three), lambda t, s: (t, 0, 0, 0)),
                pl.BlockSpec((1, heads, tokens, tokens), lambda t, s: (t, 0, 0, 0)),
                pl.BlockSpec(memory_space=pl.ANY),
            ],
            out_specs=pl.BlockSpec((1, tokens, heads, three), lambda t, s: (t, 0, 0, 0)),
            scratch_shapes=[
                pltpu.VMEM((1, 4, block, cols), BF16),
                pltpu.VMEM((rows, cols), BF16),
                pltpu.VMEM((heads, tokens, three), BF16),
                pltpu.SemaphoreType.DMA,
            ],
        ),
        out_shape=jax.ShapeDtypeStruct((tiles, tokens, heads, three), BF16),
        compiler_params=params(),
        cost_estimate=pl.CostEstimate(
            flops=8 * tiles * heads * tokens * tokens * 128 * 4, bytes_accessed=15_000_000, transcendentals=0
        ),
        name="backward",
    )(scal, *pieces, acc, qkv, probs, weight)


def reduce_peers(keep, send, shift_y, flip_core, flip_z):
    got = lax.ppermute(send, "dp", flip_core)
    width = keep.shape[2]
    mine = keep.astype(F32) + got.astype(F32)
    mine = mine.reshape(4, 2, -1, width)
    parts = [mine[0]] + [
        lax.ppermute(mine[s].astype(BF16), "dp", shift_y(s)).astype(F32) for s in (1, 3, 2)
    ]
    total = parts[0] + parts[1] + parts[2] + parts[3]
    last = lax.ppermute(total[1].astype(BF16), "dp", flip_z)
    return total[0] + last.astype(F32)


def body(cuts, projections, cotangent, out_weight, tile_counts, fragment, drift):
    dp_size = lax.axis_size("dp")
    fsdp_size = lax.axis_size("fsdp")
    rep_size = lax.axis_size("rep")
    heads, hd, width = out_weight.shape
    me = lax.axis_index("dp")
    core, y, z = me % 2, (me // 2) % 4, me // 8

    def flip_core():
        return [(i, i ^ 1) for i in range(dp_size)]

    def flip_z():
        return [(i, i ^ 8) for i in range(dp_size)]

    def shift_y(s):
        return [(i, (i // 8) * 8 + ((i // 2 + s) % 4) * 2 + i % 2) for i in range(dp_size)]

    def shift_x(s):
        return [(i, (i + s) % fsdp_size) for i in range(fsdp_size)]

    def shift_rep(s):
        return [(i, (i + s) % rep_size) for i in range(rep_size)]

    slots = [
        (z ^ dz) * 8 + ((y + dy) % 4) * 2 + (core ^ dc) for dc in range(2) for dy in range(4) for dz in range(2)
    ]
    scal = jnp.stack([tile_counts[0, me], lax.axis_index("fsdp"), *slots]).astype(jnp.int32)

    weight = out_weight.reshape(heads * hd, width)
    qkv, probs, ctx = forward(scal, projections)

    frag_width = width // FRAGS
    picked = lax.dynamic_slice_in_dim(drift[0], fragment[0] * frag_width, frag_width, 2)
    low = picked.astype(BF16)
    others = [lax.ppermute(low, "rep", shift_rep(s)).astype(F32) for s in range(1, rep_size)]
    synced = (low.astype(F32) + others[0] + others[1] + others[2]) / rep_size

    acc = None
    reduced = []
    for i, (start, stop) in enumerate(cuts):
        own = cotangent[:, :, start:stop]
        minus1 = lax.ppermute(own, "fsdp", shift_x(1))
        plus1 = lax.ppermute(own, "fsdp", shift_x(-1))
        if i % 2 == 0:
            plus2 = lax.ppermute(plus1, "fsdp", shift_x(-1))
        else:
            plus2 = lax.ppermute(minus1, "fsdp", shift_x(1))
        pieces = (own, plus1, plus2, minus1)
        last = i == len(cuts) - 1
        keep, send, *rest = chunk(scal, pieces, ctx, weight, acc, start, i == 0, not last)
        if not last:
            acc = rest[0]
        reduced.append(reduce_peers(keep, send, shift_y, flip_core(), flip_z()))
    gradients = backward(scal, pieces, acc, qkv, probs, weight, cuts[-1][0])
    weight_grad = jnp.concatenate(reduced, axis=1) / (CAP * dp_size)
    return gradients, weight_grad.reshape(drift.shape), synced


def solution(mesh):
    sizes = [4, 4, 4, 4, 5, 4]
    edges = [0]
    for size in sizes:
        edges.append(edges[-1] + size * LANES)
    cuts = list(zip(edges[:-1], edges[1:]))
    return jax.shard_map(
        functools.partial(body, cuts),
        mesh=mesh,
        in_specs=(
            P(("rep", "dp"), None, "fsdp", None),
            P(("rep", "dp"), "fsdp", None),
            P("fsdp", None, None),
            P("rep", None),
            P(),
            P("rep", "fsdp", "dp", None),
        ),
        out_specs=(
            P(("rep", "dp"), None, "fsdp", None),
            P("rep", "fsdp", "dp", None),
            P("fsdp", "dp", None),
        ),
        check_vma=False,
    )
```

```python
import functools

import jax
import jax.numpy as jnp
from jax import lax
from jax.experimental import pallas as pl
from jax.experimental.pallas import tpu as pltpu
from jax.sharding import PartitionSpec as P

CAP = 6
FRAGS = 5
LANES = 128
VMEM_LIMIT = 56 * 1024 * 1024
F32 = jnp.float32
BF16 = jnp.bfloat16

NT = (((1,), (1,)), ((), ()))
TN = (((0,), (0,)), ((), ()))


def vmem():
    return pl.BlockSpec(memory_space=pltpu.VMEM)


def params(**extra):
    return pltpu.CompilerParams(vmem_limit_bytes=VMEM_LIMIT, **extra)


def forward_kernel(scal, proj, qkv_out, probs_out, ctx_out, wide):
    heads, tokens, three = qkv_out.shape[1:]
    hd = three // 3
    factor = hd ** (-0.5)
    live = pl.program_id(0) < scal[0]
    qkv = jnp.swapaxes(proj[0], 0, 1)
    qkv_out[0] = qkv
    q, k, v = (qkv[:, :, n * hd : (n + 1) * hd] for n in range(3))
    scores = [lax.dot_general(k[h], q[h], NT, preferred_element_type=F32) for h in range(heads)]
    scores = jnp.stack(scores) * factor
    shifted = jnp.exp(scores - jnp.max(scores, axis=1, keepdims=True))
    probs = shifted * (1.0 / jnp.sum(shifted, axis=1, keepdims=True))
    probs_out[0] = probs
    low = probs.astype(BF16)
    context = [lax.dot_general(v[h], low[h], TN, preferred_element_type=F32) for h in range(heads)]
    for h in range(heads):
        wide[h] = jnp.where(live, context[h], 0.0)
    slots = scal.shape[0] - 2
    for j in range(slots):
        row = pl.multiple_of(scal[2 + j] * 8, 8)
        rows = jnp.concatenate([wide[h, pl.ds(row, 8), :] for h in range(heads)], axis=0)
        ctx_out[j * 8 * heads : (j + 1) * 8 * heads, :] = rows.astype(BF16)


def forward(scal, projections):
    tiles, tokens, heads, three = projections.shape
    hd = three // 3
    return pl.pallas_call(
        forward_kernel,
        grid_spec=pltpu.PrefetchScalarGridSpec(
            num_scalar_prefetch=1,
            grid=(tiles,),
            in_specs=[pl.BlockSpec((1, tokens, heads, three), lambda t, s: (t, 0, 0, 0))],
            out_specs=[
                pl.BlockSpec((1, heads, tokens, three), lambda t, s: (t, 0, 0, 0)),
                pl.BlockSpec((1, heads, tokens, tokens), lambda t, s: (t, 0, 0, 0)),
                pl.BlockSpec((heads * hd, tokens), lambda t, s: (0, t)),
            ],
            scratch_shapes=[pltpu.VMEM((heads, hd, tokens), F32)],
        ),
        out_shape=[
            jax.ShapeDtypeStruct((tiles, heads, tokens, three), BF16),
            jax.ShapeDtypeStruct((tiles, heads, tokens, tokens), F32),
            jax.ShapeDtypeStruct((heads * hd, tiles * tokens), BF16),
        ],
        compiler_params=params(),
        cost_estimate=pl.CostEstimate(
            flops=4 * tiles * heads * tokens * tokens * hd * 4, bytes_accessed=12_000_000, transcendentals=0
        ),
        name="forward",
    )(scal, projections)


def gather_copies(me, pieces, gathered, sem):
    own, plus1, plus2_low, plus2_high, minus1 = pieces
    low = plus2_low.shape[0]

    def copy(n, src, step, tiles=slice(None)):
        return pltpu.make_async_copy(src, gathered.at[tiles, lax.rem(me + step, 4)], sem(n))

    return [
        copy(0, own, 0),
        copy(1, plus1, 1),
        copy(2, plus2_low, 2, pl.ds(0, low)),
        copy(3, plus2_high, 2, pl.ds(low, plus2_high.shape[0])),
        copy(4, minus1, 3),
    ]


def sums_kernel(scal, own, plus1, plus2_low, plus2_high, minus1, ctx, keep, send, gathered, ctx_part, sums, sems):
    tiles, _, tokens, cols = gathered.shape
    loads = [pltpu.make_async_copy(ctx, ctx_part, sems.at[5])]
    loads += gather_copies(scal[1], (own, plus1, plus2_low, plus2_high, minus1), gathered, lambda n: sems.at[n])
    for c in loads:
        c.start()
    for c in loads:
        c.wait()
    step = 2 * LANES
    half = keep.shape[0]
    stores = []
    for low in range(0, cols, step):
        high = min(low + step, cols)
        cot = gathered[:, :, :, low:high].reshape(tiles * 4 * tokens, high - low)
        part = jnp.dot(ctx_part[...], cot, preferred_element_type=F32)
        sums[:, :, low:high] = part.astype(BF16).reshape(sums.shape[0], sums.shape[1], high - low)
    stores = [
        pltpu.make_async_copy(sums.at[half:], send, sems.at[6]),
        pltpu.make_async_copy(sums.at[:half], keep, sems.at[7]),
    ]
    for c in stores:
        c.start()
    for c in stores:
        c.wait()


def weight_sums(scal, pieces, ctx):
    tiles, tokens, cols = pieces[0].shape
    rows, depth = ctx.shape
    any_spec = pl.BlockSpec(memory_space=pl.ANY)
    return pl.pallas_call(
        sums_kernel,
        in_specs=[pl.BlockSpec(memory_space=pltpu.SMEM)] + [any_spec] * 6,
        out_specs=[any_spec] * 2,
        out_shape=[jax.ShapeDtypeStruct((8, rows // 16, cols), BF16)] * 2,
        scratch_shapes=[
            pltpu.VMEM((tiles, 4, tokens, cols), BF16),
            pltpu.VMEM((rows, depth), BF16),
            pltpu.VMEM((16, rows // 16, cols), BF16),
            pltpu.SemaphoreType.DMA((8,)),
        ],
        compiler_params=params(),
        cost_estimate=pl.CostEstimate(flops=8_000_000_000, bytes_accessed=1000, transcendentals=0),
        name="weight_sums",
    )(scal, *pieces, ctx)


def ctx_grad_kernel(groups, cuts, scal, weight, *rest):
    pieces, rest = rest[: 5 * groups], rest[5 * groups :]
    out, gathered, (w, acc, low_acc, sems) = rest[0], rest[1 : 1 + groups], rest[1 + groups :]
    loads = []
    for g, (start, stop) in enumerate(cuts):
        sem = lambda n, g=g: sems.at[6 * g + n]
        cols = pltpu.make_async_copy(weight.at[:, start:stop], w.at[:, start:stop], sem(5))
        loads.append(gather_copies(scal[1], pieces[5 * g : 5 * g + 5], gathered[g], sem) + [cols])
        for c in loads[-1]:
            c.start()
    tiles, blocks, tokens, _ = gathered[0].shape
    rows = tiles * blocks * tokens
    step = rows // 3
    for g, (start, stop) in enumerate(cuts):
        for c in loads[g]:
            c.wait()
        for n in range(3):
            cot = gathered[g][n * (tiles // 3) : (n + 1) * (tiles // 3)].reshape(step, stop - start)
            part = lax.dot_general(cot, w[:, start:stop], NT, preferred_element_type=F32)
            at = slice(n * step, (n + 1) * step)
            part = part if g == 0 else acc[at, :] + part
            if g < groups - 1:
                acc[at, :] = part
            else:
                low_acc[at, :] = part.astype(BF16)
    store = pltpu.make_async_copy(low_acc, out, sems.at[6 * groups])
    store.start()
    store.wait()


def context_gradient(scal, weight, pieces, cuts):
    groups = len(cuts)
    tiles, tokens, _ = pieces[0][0].shape
    rows, width = weight.shape
    depth = tiles * 4 * tokens
    any_spec = pl.BlockSpec(memory_space=pl.ANY)
    return pl.pallas_call(
        functools.partial(ctx_grad_kernel, groups, cuts),
        in_specs=[pl.BlockSpec(memory_space=pltpu.SMEM)] + [any_spec] * (1 + 5 * groups),
        out_specs=any_spec,
        out_shape=jax.ShapeDtypeStruct((depth, rows), BF16),
        scratch_shapes=[pltpu.VMEM((tiles, 4, tokens, stop - start), BF16) for start, stop in cuts]
        + [
            pltpu.VMEM((rows, width), BF16),
            pltpu.VMEM((depth, rows), F32),
            pltpu.VMEM((depth, rows), BF16),
            pltpu.SemaphoreType.DMA((6 * groups + 1,)),
        ],
        compiler_params=params(),
        cost_estimate=pl.CostEstimate(flops=8_000_000_000, bytes_accessed=1000, transcendentals=0),
        name="context_gradient",
    )(scal, weight, *[p for some in pieces for p in some])


def backward_kernel(scal, ctx_grad, qkv, probs, out, ctx_grad_v, qkv_v, probs_v, out_v, grads, sems):
    tiles, heads, tokens, three = qkv_v.shape
    hd = three // 3
    factor = hd ** (-0.5)

    def loads(t):
        rows = pl.ds(pl.multiple_of(t * tokens, tokens), tokens)
        return [
            pltpu.make_async_copy(ctx_grad.at[rows], ctx_grad_v.at[rows], sems.at[0, t]),
            pltpu.make_async_copy(qkv.at[t], qkv_v.at[t], sems.at[1, t]),
            pltpu.make_async_copy(probs.at[t], probs_v.at[t], sems.at[2, t]),
        ]

    def store(t):
        return pltpu.make_async_copy(out_v.at[t], out.at[t], sems.at[3, t])

    for t in range(tiles):
        for c in loads(t):
            c.start()

    def one_tile(t, carry):
        for c in loads(t):
            c.wait()

        @pl.when(t < scal[0])
        def _():
            rows = pl.ds(pl.multiple_of(t * tokens, tokens), tokens)
            q, k, v = (qkv_v[t, :, :, n * hd : (n + 1) * hd] for n in range(3))
            dctx = [ctx_grad_v[rows, h * hd : (h + 1) * hd] for h in range(heads)]
            probs_wide = probs_v[t]
            low = probs_wide.astype(BF16)
            prob_grad = [lax.dot_general(v[h], dctx[h], NT, preferred_element_type=F32) for h in range(heads)]
            value_grad = [jnp.dot(low[h], dctx[h], preferred_element_type=F32) for h in range(heads)]
            prob_grad = jnp.stack(prob_grad)
            centre = jnp.sum(probs_wide * prob_grad, axis=1, keepdims=True)
            score_grad = (probs_wide * (prob_grad - centre) * factor).astype(BF16)
            key_grad = [jnp.dot(score_grad[h], q[h], preferred_element_type=F32) for h in range(heads)]
            query_grad = [
                lax.dot_general(score_grad[h], k[h], TN, preferred_element_type=F32) for h in range(heads)
            ]
            for h in range(heads):
                grads[h, :, 0:hd] = query_grad[h].astype(BF16)
                grads[h, :, hd : 2 * hd] = key_grad[h].astype(BF16)
                grads[h, :, 2 * hd : 3 * hd] = value_grad[h].astype(BF16)
            out_v[t] = jnp.swapaxes(grads[...], 0, 1)

        @pl.when(t >= scal[0])
        def _():
            out_v[t] = jnp.zeros(out_v.shape[1:], BF16)

        store(t).start()
        return carry

    lax.fori_loop(0, tiles, one_tile, 0)
    for t in range(tiles):
        store(t).wait()


def backward(scal, ctx_grad, qkv, probs):
    tiles, heads, tokens, three = qkv.shape
    any_spec = pl.BlockSpec(memory_space=pl.ANY)
    return pl.pallas_call(
        backward_kernel,
        in_specs=[pl.BlockSpec(memory_space=pltpu.SMEM)] + [any_spec] * 3,
        out_specs=any_spec,
        out_shape=jax.ShapeDtypeStruct((tiles, tokens, heads, three), BF16),
        scratch_shapes=[
            pltpu.VMEM(ctx_grad.shape, BF16),
            pltpu.VMEM(qkv.shape, BF16),
            pltpu.VMEM(probs.shape, F32),
            pltpu.VMEM((tiles, tokens, heads, three), BF16),
            pltpu.VMEM((heads, tokens, three), BF16),
            pltpu.SemaphoreType.DMA((4, tiles)),
        ],
        compiler_params=params(),
        cost_estimate=pl.CostEstimate(flops=8_000_000_000, bytes_accessed=1000, transcendentals=0),
        name="backward",
    )(scal, ctx_grad, qkv, probs)


def body(cuts, projections, cotangent, out_weight, tile_counts, fragment, drift):
    dp_size = lax.axis_size("dp")
    fsdp_size = lax.axis_size("fsdp")
    rep_size = lax.axis_size("rep")
    heads, hd, width = out_weight.shape
    me = lax.axis_index("dp")
    core = me % 2

    def flip_core():
        return [(i, i ^ 1) for i in range(dp_size)]

    def shift_x(s):
        return [(i, (i + s) % fsdp_size) for i in range(fsdp_size)]

    slots = [2 * k + (core ^ dc) for dc in range(2) for k in range(dp_size // 2)]
    same_core = [list(range(c, dp_size, 2)) for c in range(2)]
    scal = jnp.stack([tile_counts[0, me], lax.axis_index("fsdp"), *slots]).astype(jnp.int32)

    weight = out_weight.reshape(heads * hd, width)
    n = len(cuts)
    tiles = projections.shape[0]
    st = dict(cot=cotangent)

    def fence(*names):
        flat, tree = jax.tree.flatten({name: st[name] for name in names})
        st.update(jax.tree.unflatten(tree, lax.optimization_barrier(flat)))

    def send_own(i):
        start, stop = cuts[i]
        st[f"own{i}"] = st["cot"][:, :, start:stop]
        st[f"near{i}"] = (
            lax.ppermute(st[f"own{i}"], "fsdp", shift_x(-1)),
            lax.ppermute(st[f"own{i}"], "fsdp", shift_x(1)),
        )

    def pass_on(i):
        split = (tiles + i % 2) // 2
        plus1, minus1 = st[f"near{i}"]
        st[f"far{i}"] = (
            lax.ppermute(plus1[:split], "fsdp", shift_x(-1)),
            lax.ppermute(minus1[split:], "fsdp", shift_x(1)),
        )

    def pieces(i):
        plus1, minus1 = st[f"near{i}"]
        return (st[f"own{i}"], plus1, *st[f"far{i}"], minus1)

    def sum_chunk(i):
        st[f"keep{i}"], st[f"send{i}"] = weight_sums(scal, pieces(i), st["ctx"])

    def cross_core(i):
        st[f"core{i}"] = lax.ppermute(st[f"send{i}"], "dp", flip_core())

    def cross_chips(*some):
        both = [(st[f"keep{i}"].astype(F32) + st[f"core{i}"].astype(F32)).astype(BF16) for i in some]
        both = jnp.concatenate(both, axis=2)
        return lax.all_to_all(both, "dp", 0, 0, axis_index_groups=same_core, tiled=True)

    send_own(0)
    send_own(1)
    qkv, probs, st["ctx"] = forward(scal, projections)
    frag_width = width // FRAGS
    picked = lax.dynamic_slice_in_dim(drift[0], fragment[0] * frag_width, frag_width, 2).astype(BF16)
    every = jnp.broadcast_to(picked[None], (rep_size, *picked.shape))
    st["drift"] = lax.all_to_all(every, "rep", 0, 0, tiled=True)
    fence("ctx", "drift", "near0", "cot")
    pass_on(0)
    send_own(2)
    fence("ctx", "near1", "far0")
    pass_on(1)
    sum_chunk(0)
    fence("ctx", "near2", "far1", "keep0", "send0")
    pass_on(2)
    cross_core(0)
    sum_chunk(1)
    fence("ctx", "far2", "keep0", "core0", "keep1", "send1")
    cross_core(1)
    sum_chunk(2)
    fence("keep0", "core0", "keep1", "core1", "keep2", "send2", "far2")
    cross_core(2)
    summed = cross_chips(0, 1, 2)
    ctx_grad = context_gradient(scal, weight, [pieces(i) for i in range(n)], cuts)
    gradients = backward(scal, ctx_grad, qkv, probs)
    weight_grad = jnp.sum(summed.astype(F32), axis=0) / (CAP * dp_size)
    synced = jnp.sum(st["drift"].astype(F32), axis=0) / rep_size
    return gradients, weight_grad.reshape(drift.shape), synced


def solution(mesh):
    sizes = [9, 10, 6]
    edges = [0]
    for size in sizes:
        edges.append(edges[-1] + size * LANES)
    cuts = list(zip(edges[:-1], edges[1:]))
    return jax.shard_map(
        functools.partial(body, cuts),
        mesh=mesh,
        in_specs=(
            P(("rep", "dp"), None, "fsdp", None),
            P(("rep", "dp"), "fsdp", None),
            P("fsdp", None, None),
            P("rep", None),
            P(),
            P("rep", "fsdp", "dp", None),
        ),
        out_specs=(
            P(("rep", "dp"), None, "fsdp", None),
            P("rep", "fsdp", "dp", None),
            P("fsdp", "dp", None),
        ),
        check_vma=False,
    )
```

```python
import functools

import jax
import jax.numpy as jnp
from jax import lax
from jax.experimental import pallas as pl
from jax.experimental.pallas import tpu as pltpu
from jax.sharding import PartitionSpec as P

CAP = 6
FRAGS = 5
LANES = 128
LARGE, SMALL = 56 * 1024 * 1024, 20 * 1024 * 1024
F32 = jnp.float32
BF16 = jnp.bfloat16

NT = (((1,), (1,)), ((), ()))
TN = (((0,), (0,)), ((), ()))


def vmem():
    return pl.BlockSpec(memory_space=pltpu.VMEM)


def params(limit):
    return pltpu.CompilerParams(vmem_limit_bytes=limit)


def forward_kernel(scal, proj, qkv_out, probs_out, ctx_out, wide):
    heads, tokens, three = qkv_out.shape[1:]
    hd = three // 3
    factor = hd ** (-0.5)
    live = pl.program_id(0) < scal[0]
    qkv = jnp.swapaxes(proj[0], 0, 1)
    qkv_out[0] = qkv
    q, k, v = (qkv[:, :, n * hd : (n + 1) * hd] for n in range(3))
    scores = [lax.dot_general(k[h], q[h], NT, preferred_element_type=F32) for h in range(heads)]
    scores = jnp.stack(scores) * factor
    shifted = jnp.exp(scores - jnp.max(scores, axis=1, keepdims=True))
    probs = shifted * (1.0 / jnp.sum(shifted, axis=1, keepdims=True))
    probs_out[0] = probs
    low = probs.astype(BF16)
    context = [lax.dot_general(v[h], low[h], TN, preferred_element_type=F32) for h in range(heads)]
    for h in range(heads):
        wide[h] = jnp.where(live, context[h], 0.0)
    slots = scal.shape[0] - 2
    for j in range(slots):
        row = pl.multiple_of(scal[2 + j] * 8, 8)
        rows = jnp.concatenate([wide[h, pl.ds(row, 8), :] for h in range(heads)], axis=0)
        ctx_out[j * 8 * heads : (j + 1) * 8 * heads, :] = rows.astype(BF16)


def forward(scal, projections):
    tiles, tokens, heads, three = projections.shape
    hd = three // 3
    return pl.pallas_call(
        forward_kernel,
        grid_spec=pltpu.PrefetchScalarGridSpec(
            num_scalar_prefetch=1,
            grid=(tiles,),
            in_specs=[pl.BlockSpec((1, tokens, heads, three), lambda t, s: (t, 0, 0, 0))],
            out_specs=[
                pl.BlockSpec((1, heads, tokens, three), lambda t, s: (t, 0, 0, 0)),
                pl.BlockSpec((1, heads, tokens, tokens), lambda t, s: (t, 0, 0, 0)),
                pl.BlockSpec((heads * hd, tokens), lambda t, s: (0, t)),
            ],
            scratch_shapes=[pltpu.VMEM((heads, hd, tokens), F32)],
        ),
        out_shape=[
            jax.ShapeDtypeStruct((tiles, heads, tokens, three), BF16),
            jax.ShapeDtypeStruct((tiles, heads, tokens, tokens), F32),
            jax.ShapeDtypeStruct((heads * hd, tiles * tokens), BF16),
        ],
        compiler_params=params(LARGE),
        cost_estimate=pl.CostEstimate(
            flops=4 * tiles * heads * tokens * tokens * hd * 4, bytes_accessed=12_000_000, transcendentals=0
        ),
        name="forward",
    )(scal, projections)


def gather_copies(me, pieces, gathered, sem):
    own, plus1, plus2_low, plus2_high, minus1 = pieces
    low = plus2_low.shape[0]

    def copy(n, src, step, tiles=slice(None)):
        return pltpu.make_async_copy(src, gathered.at[tiles, lax.rem(me + step, 4)], sem(n))

    return [
        copy(0, own, 0),
        copy(1, plus1, 1),
        copy(2, plus2_low, 2, pl.ds(0, low)),
        copy(3, plus2_high, 2, pl.ds(low, plus2_high.shape[0])),
        copy(4, minus1, 3),
    ]


def column_parts(cols):
    middle = (cols // LANES + 1) // 2 * LANES
    return [(0, middle), (middle, cols)]


def sums_kernel(scal, own, plus1, plus2_low, plus2_high, minus1, ctx, keep, send, gathered, ctx_part, sums, sems):
    tiles, _, tokens, cols = gathered.shape
    parts = column_parts(cols)
    half = keep.shape[0]
    first = pltpu.make_async_copy(ctx, ctx_part, sems.at[0, 5])
    first.start()
    loads = []
    for n, (low, high) in enumerate(parts):
        sides = [r.at[:, :, low:high] for r in (own, plus1, plus2_low, plus2_high, minus1)]
        loads.append(
            gather_copies(scal[1], sides, gathered.at[:, :, :, low:high], lambda m, n=n: sems.at[n, m])
        )
        for c in loads[-1]:
            c.start()
    first.wait()
    stores = []
    for n, (low, high) in enumerate(parts):
        for c in loads[n]:
            c.wait()
        cot = gathered[:, :, :, low:high].reshape(tiles * 4 * tokens, high - low)
        for m, (out, at) in enumerate([(send, half), (keep, 0)]):
            rows = half * sums.shape[1]
            mine = ctx_part[at * sums.shape[1] : at * sums.shape[1] + rows, :]
            part = jnp.dot(mine, cot, preferred_element_type=F32)
            sums[at : at + half, :, low:high] = part.astype(BF16).reshape(half, sums.shape[1], high - low)
            stores.append(
                pltpu.make_async_copy(
                    sums.at[at : at + half, :, low:high], out.at[:, :, low:high], sems.at[n, 6 + m]
                )
            )
            stores[-1].start()
    for c in stores:
        c.wait()


def weight_sums(scal, pieces, ctx):
    tiles, tokens, cols = pieces[0].shape
    rows, depth = ctx.shape
    any_spec = pl.BlockSpec(memory_space=pl.ANY)
    return pl.pallas_call(
        sums_kernel,
        in_specs=[pl.BlockSpec(memory_space=pltpu.SMEM)] + [any_spec] * 6,
        out_specs=[any_spec] * 2,
        out_shape=[jax.ShapeDtypeStruct((8, rows // 16, cols), BF16)] * 2,
        scratch_shapes=[
            pltpu.VMEM((tiles, 4, tokens, cols), BF16),
            pltpu.VMEM((rows, depth), BF16),
            pltpu.VMEM((16, rows // 16, cols), BF16),
            pltpu.SemaphoreType.DMA((2, 8)),
        ],
        compiler_params=params(SMALL),
        cost_estimate=pl.CostEstimate(flops=8_000_000_000, bytes_accessed=1000, transcendentals=0),
        name="weight_sums",
    )(scal, *pieces, ctx)


def ctx_grad_kernel(groups, cuts, scal, weight, *rest):
    pieces, rest = rest[: 5 * groups], rest[5 * groups :]
    out, gathered, (w, acc, low_acc, sems) = rest[0], rest[1 : 1 + groups], rest[1 + groups :]
    loads = []
    for g, (start, stop) in enumerate(cuts):
        sem = lambda n, g=g: sems.at[6 * g + n]
        cols = pltpu.make_async_copy(weight.at[:, start:stop], w.at[:, start:stop], sem(5))
        loads.append(gather_copies(scal[1], pieces[5 * g : 5 * g + 5], gathered[g], sem) + [cols])
        for c in loads[-1]:
            c.start()
    tiles, blocks, tokens, _ = gathered[0].shape
    rows = tiles * blocks * tokens
    step = rows // 3
    for g, (start, stop) in enumerate(cuts):
        for c in loads[g]:
            c.wait()
        for n in range(3):
            cot = gathered[g][n * (tiles // 3) : (n + 1) * (tiles // 3)].reshape(step, stop - start)
            part = lax.dot_general(cot, w[:, start:stop], NT, preferred_element_type=F32)
            at = slice(n * step, (n + 1) * step)
            part = part if g == 0 else acc[at, :] + part
            if g < groups - 1:
                acc[at, :] = part
            else:
                low_acc[at, :] = part.astype(BF16)
    store = pltpu.make_async_copy(low_acc, out, sems.at[6 * groups])
    store.start()
    store.wait()


def context_gradient(scal, weight, pieces, cuts):
    groups = len(cuts)
    tiles, tokens, _ = pieces[0][0].shape
    rows, width = weight.shape
    depth = tiles * 4 * tokens
    any_spec = pl.BlockSpec(memory_space=pl.ANY)
    return pl.pallas_call(
        functools.partial(ctx_grad_kernel, groups, cuts),
        in_specs=[pl.BlockSpec(memory_space=pltpu.SMEM)] + [any_spec] * (1 + 5 * groups),
        out_specs=any_spec,
        out_shape=jax.ShapeDtypeStruct((depth, rows), BF16),
        scratch_shapes=[pltpu.VMEM((tiles, 4, tokens, stop - start), BF16) for start, stop in cuts]
        + [
            pltpu.VMEM((rows, width), BF16),
            pltpu.VMEM((depth, rows), F32),
            pltpu.VMEM((depth, rows), BF16),
            pltpu.SemaphoreType.DMA((6 * groups + 1,)),
        ],
        compiler_params=params(LARGE),
        cost_estimate=pl.CostEstimate(flops=8_000_000_000, bytes_accessed=1000, transcendentals=0),
        name="context_gradient",
    )(scal, weight, *[p for some in pieces for p in some])


def backward_kernel(scal, ctx_grad, qkv, probs, out, ctx_grad_v, qkv_v, probs_v, out_v, grads, sems):
    tiles, heads, tokens, three = qkv_v.shape
    hd = three // 3
    factor = hd ** (-0.5)

    def loads(t):
        rows = pl.ds(pl.multiple_of(t * tokens, tokens), tokens)
        return [
            pltpu.make_async_copy(ctx_grad.at[rows], ctx_grad_v.at[rows], sems.at[0, t]),
            pltpu.make_async_copy(qkv.at[t], qkv_v.at[t], sems.at[1, t]),
            pltpu.make_async_copy(probs.at[t], probs_v.at[t], sems.at[2, t]),
        ]

    def store(t):
        return pltpu.make_async_copy(out_v.at[t], out.at[t], sems.at[3, t])

    for t in range(tiles):
        for c in loads(t):
            c.start()

    def one_tile(t, carry):
        for c in loads(t):
            c.wait()

        @pl.when(t < scal[0])
        def _():
            rows = pl.ds(pl.multiple_of(t * tokens, tokens), tokens)
            q, k, v = (qkv_v[t, :, :, n * hd : (n + 1) * hd] for n in range(3))
            dctx = [ctx_grad_v[rows, h * hd : (h + 1) * hd] for h in range(heads)]
            probs_wide = probs_v[t]
            low = probs_wide.astype(BF16)
            prob_grad = [lax.dot_general(v[h], dctx[h], NT, preferred_element_type=F32) for h in range(heads)]
            value_grad = [jnp.dot(low[h], dctx[h], preferred_element_type=F32) for h in range(heads)]
            prob_grad = jnp.stack(prob_grad)
            centre = jnp.sum(probs_wide * prob_grad, axis=1, keepdims=True)
            score_grad = (probs_wide * (prob_grad - centre) * factor).astype(BF16)
            key_grad = [jnp.dot(score_grad[h], q[h], preferred_element_type=F32) for h in range(heads)]
            query_grad = [
                lax.dot_general(score_grad[h], k[h], TN, preferred_element_type=F32) for h in range(heads)
            ]
            for h in range(heads):
                grads[h, :, 0:hd] = query_grad[h].astype(BF16)
                grads[h, :, hd : 2 * hd] = key_grad[h].astype(BF16)
                grads[h, :, 2 * hd : 3 * hd] = value_grad[h].astype(BF16)
            out_v[t] = jnp.swapaxes(grads[...], 0, 1)

        @pl.when(t >= scal[0])
        def _():
            out_v[t] = jnp.zeros(out_v.shape[1:], BF16)

        store(t).start()
        return carry

    lax.fori_loop(0, tiles, one_tile, 0)
    for t in range(tiles):
        store(t).wait()


def backward(scal, ctx_grad, qkv, probs):
    tiles, heads, tokens, three = qkv.shape
    any_spec = pl.BlockSpec(memory_space=pl.ANY)
    return pl.pallas_call(
        backward_kernel,
        in_specs=[pl.BlockSpec(memory_space=pltpu.SMEM)] + [any_spec] * 3,
        out_specs=any_spec,
        out_shape=jax.ShapeDtypeStruct((tiles, tokens, heads, three), BF16),
        scratch_shapes=[
            pltpu.VMEM(ctx_grad.shape, BF16),
            pltpu.VMEM(qkv.shape, BF16),
            pltpu.VMEM(probs.shape, F32),
            pltpu.VMEM((tiles, tokens, heads, three), BF16),
            pltpu.VMEM((heads, tokens, three), BF16),
            pltpu.SemaphoreType.DMA((4, tiles)),
        ],
        compiler_params=params(LARGE),
        cost_estimate=pl.CostEstimate(flops=8_000_000_000, bytes_accessed=1000, transcendentals=0),
        name="backward",
    )(scal, ctx_grad, qkv, probs)


def body(cuts, projections, cotangent, out_weight, tile_counts, fragment, drift):
    dp_size = lax.axis_size("dp")
    fsdp_size = lax.axis_size("fsdp")
    rep_size = lax.axis_size("rep")
    heads, hd, width = out_weight.shape
    me = lax.axis_index("dp")
    core = me % 2

    def flip_core():
        return [(i, i ^ 1) for i in range(dp_size)]

    def shift_x(s):
        return [(i, (i + s) % fsdp_size) for i in range(fsdp_size)]

    slots = [2 * k + (core ^ dc) for dc in range(2) for k in range(dp_size // 2)]
    same_core = [list(range(c, dp_size, 2)) for c in range(2)]
    scal = jnp.stack([tile_counts[0, me], lax.axis_index("fsdp"), *slots]).astype(jnp.int32)

    weight = out_weight.reshape(heads * hd, width)
    n = len(cuts)
    tiles = projections.shape[0]
    st = dict(cot=cotangent)

    def fence(*names):
        flat, tree = jax.tree.flatten({name: st[name] for name in names})
        st.update(jax.tree.unflatten(tree, lax.optimization_barrier(flat)))

    def send_own(i):
        start, stop = cuts[i]
        st[f"own{i}"] = st["cot"][:, :, start:stop]
        st[f"near{i}"] = (
            lax.ppermute(st[f"own{i}"], "fsdp", shift_x(-1)),
            lax.ppermute(st[f"own{i}"], "fsdp", shift_x(1)),
        )

    def pass_on(i):
        split = (tiles + i % 2) // 2
        plus1, minus1 = st[f"near{i}"]
        st[f"far{i}"] = (
            lax.ppermute(plus1[:split], "fsdp", shift_x(-1)),
            lax.ppermute(minus1[split:], "fsdp", shift_x(1)),
        )

    def pieces(i):
        plus1, minus1 = st[f"near{i}"]
        return (st[f"own{i}"], plus1, *st[f"far{i}"], minus1)

    def sum_chunk(i):
        st[f"keep{i}"], st[f"send{i}"] = weight_sums(scal, pieces(i), st["ctx"])

    def cross_core(i):
        st[f"core{i}"] = lax.ppermute(st[f"send{i}"], "dp", flip_core())

    def cross_chips(*some):
        both = [(st[f"keep{i}"].astype(F32) + st[f"core{i}"].astype(F32)).astype(BF16) for i in some]
        both = jnp.concatenate(both, axis=2)
        return lax.all_to_all(both, "dp", 0, 0, axis_index_groups=same_core, tiled=True)

    send_own(0)
    send_own(1)
    qkv, probs, st["ctx"] = forward(scal, projections)
    frag_width = width // FRAGS
    picked = lax.dynamic_slice_in_dim(drift[0], fragment[0] * frag_width, frag_width, 2).astype(BF16)
    every = jnp.broadcast_to(picked[None], (rep_size, *picked.shape))
    st["drift"] = lax.all_to_all(every, "rep", 0, 0, tiled=True)
    fence("ctx", "drift", "near0", "cot")
    pass_on(0)
    send_own(2)
    fence("ctx", "near1", "far0")
    pass_on(1)
    sum_chunk(0)
    fence("near2", "keep0", "send0")
    pass_on(2)
    cross_core(0)
    fence("ctx", "far1")
    sum_chunk(1)
    fence("ctx", "far2", "keep0", "core0", "keep1", "send1")
    cross_core(1)
    sum_chunk(2)
    fence("keep0", "core0", "keep1", "core1", "keep2", "send2", "far2")
    cross_core(2)
    summed = [cross_chips(0, 1, 2)]
    ctx_grad = context_gradient(scal, weight, [pieces(i) for i in range(n)], cuts)
    gradients = backward(scal, ctx_grad, qkv, probs)
    weight_grad = jnp.concatenate([jnp.sum(p.astype(F32), axis=0) for p in summed], axis=1) / (CAP * dp_size)
    synced = jnp.sum(st["drift"].astype(F32), axis=0) / rep_size
    return gradients, weight_grad.reshape(drift.shape), synced


def solution(mesh):
    sizes = [8, 10, 7]
    edges = [0]
    for size in sizes:
        edges.append(edges[-1] + size * LANES)
    cuts = list(zip(edges[:-1], edges[1:]))
    return jax.shard_map(
        functools.partial(body, cuts),
        mesh=mesh,
        in_specs=(
            P(("rep", "dp"), None, "fsdp", None),
            P(("rep", "dp"), "fsdp", None),
            P("fsdp", None, None),
            P("rep", None),
            P(),
            P("rep", "fsdp", "dp", None),
        ),
        out_specs=(
            P(("rep", "dp"), None, "fsdp", None),
            P("rep", "fsdp", "dp", None),
            P("fsdp", "dp", None),
        ),
        check_vma=False,
    )
```

```python
import functools

import jax
import jax.numpy as jnp
from jax import lax
from jax.experimental import pallas as pl
from jax.experimental.pallas import tpu as pltpu
from jax.sharding import PartitionSpec as P

CAP = 6
FRAGS = 5
LANES = 128
LARGE, SMALL = 56 * 1024 * 1024, 20 * 1024 * 1024
F32 = jnp.float32
BF16 = jnp.bfloat16

NT = (((1,), (1,)), ((), ()))
TN = (((0,), (0,)), ((), ()))


def vmem():
    return pl.BlockSpec(memory_space=pltpu.VMEM)


def params(limit):
    return pltpu.CompilerParams(vmem_limit_bytes=limit)


def forward_kernel(scal, proj, qkv_out, probs_out, ctx_out, wide):
    heads, tokens, three = qkv_out.shape[1:]
    hd = three // 3
    factor = hd ** (-0.5)
    live = pl.program_id(0) < scal[0]
    qkv = jnp.swapaxes(proj[0], 0, 1)
    qkv_out[0] = qkv
    q, k, v = (qkv[:, :, n * hd : (n + 1) * hd] for n in range(3))
    scores = [lax.dot_general(k[h], q[h], NT, preferred_element_type=F32) for h in range(heads)]
    scores = jnp.stack(scores) * factor
    shifted = jnp.exp(scores - jnp.max(scores, axis=1, keepdims=True))
    probs = shifted * (1.0 / jnp.sum(shifted, axis=1, keepdims=True))
    probs_out[0] = probs
    low = probs.astype(BF16)
    context = [lax.dot_general(v[h], low[h], TN, preferred_element_type=F32) for h in range(heads)]
    for h in range(heads):
        wide[h] = jnp.where(live, context[h], 0.0)
    slots = scal.shape[0] - 2
    for j in range(slots):
        row = pl.multiple_of(scal[2 + j] * 8, 8)
        rows = jnp.concatenate([wide[h, pl.ds(row, 8), :] for h in range(heads)], axis=0)
        ctx_out[j * 8 * heads : (j + 1) * 8 * heads, :] = rows.astype(BF16)


def forward(scal, projections):
    tiles, tokens, heads, three = projections.shape
    hd = three // 3
    return pl.pallas_call(
        forward_kernel,
        grid_spec=pltpu.PrefetchScalarGridSpec(
            num_scalar_prefetch=1,
            grid=(tiles,),
            in_specs=[pl.BlockSpec((1, tokens, heads, three), lambda t, s: (t, 0, 0, 0))],
            out_specs=[
                pl.BlockSpec((1, heads, tokens, three), lambda t, s: (t, 0, 0, 0)),
                pl.BlockSpec((1, heads, tokens, tokens), lambda t, s: (t, 0, 0, 0)),
                pl.BlockSpec((heads * hd, tokens), lambda t, s: (0, t)),
            ],
            scratch_shapes=[pltpu.VMEM((heads, hd, tokens), F32)],
        ),
        out_shape=[
            jax.ShapeDtypeStruct((tiles, heads, tokens, three), BF16),
            jax.ShapeDtypeStruct((tiles, heads, tokens, tokens), F32),
            jax.ShapeDtypeStruct((heads * hd, tiles * tokens), BF16),
        ],
        compiler_params=params(LARGE),
        cost_estimate=pl.CostEstimate(
            flops=4 * tiles * heads * tokens * tokens * hd * 4, bytes_accessed=12_000_000, transcendentals=0
        ),
        name="forward",
    )(scal, projections)


def gather_copies(me, pieces, gathered, sem):
    own, plus1, plus2_low, plus2_high, minus1 = pieces
    low = plus2_low.shape[0]

    def copy(n, src, step, tiles=slice(None)):
        return pltpu.make_async_copy(src, gathered.at[tiles, lax.rem(me + step, 4)], sem(n))

    return [
        copy(0, own, 0),
        copy(1, plus1, 1),
        copy(2, plus2_low, 2, pl.ds(0, low)),
        copy(3, plus2_high, 2, pl.ds(low, plus2_high.shape[0])),
        copy(4, minus1, 3),
    ]


def column_parts(cols):
    middle = (cols // LANES + 1) // 2 * LANES
    return [(0, middle), (middle, cols)]


def sums_kernel(scal, own, plus1, plus2_low, plus2_high, minus1, ctx, keep, send, gathered, ctx_part, sums, sems):
    tiles, _, tokens, cols = gathered.shape
    parts = column_parts(cols)
    half = keep.shape[0]
    first = pltpu.make_async_copy(ctx, ctx_part, sems.at[0, 5])
    first.start()
    loads = []
    for n, (low, high) in enumerate(parts):
        sides = [r.at[:, :, low:high] for r in (own, plus1, plus2_low, plus2_high, minus1)]
        loads.append(
            gather_copies(scal[1], sides, gathered.at[:, :, :, low:high], lambda m, n=n: sems.at[n, m])
        )
        for c in loads[-1]:
            c.start()
    first.wait()
    stores = []
    for n, (low, high) in enumerate(parts):
        for c in loads[n]:
            c.wait()
        cot = gathered[:, :, :, low:high].reshape(tiles * 4 * tokens, high - low)
        for m, (out, at) in enumerate([(send, half), (keep, 0)]):
            rows = half * sums.shape[1]
            mine = ctx_part[at * sums.shape[1] : at * sums.shape[1] + rows, :]
            part = jnp.dot(mine, cot, preferred_element_type=F32)
            sums[at : at + half, :, low:high] = part.astype(BF16).reshape(half, sums.shape[1], high - low)
            stores.append(
                pltpu.make_async_copy(
                    sums.at[at : at + half, :, low:high], out.at[:, :, low:high], sems.at[n, 6 + m]
                )
            )
            stores[-1].start()
    for c in stores:
        c.wait()


def weight_sums(scal, pieces, ctx):
    tiles, tokens, cols = pieces[0].shape
    rows, depth = ctx.shape
    any_spec = pl.BlockSpec(memory_space=pl.ANY)
    return pl.pallas_call(
        sums_kernel,
        in_specs=[pl.BlockSpec(memory_space=pltpu.SMEM)] + [any_spec] * 6,
        out_specs=[any_spec] * 2,
        out_shape=[jax.ShapeDtypeStruct((8, rows // 16, cols), BF16)] * 2,
        scratch_shapes=[
            pltpu.VMEM((tiles, 4, tokens, cols), BF16),
            pltpu.VMEM((rows, depth), BF16),
            pltpu.VMEM((16, rows // 16, cols), BF16),
            pltpu.SemaphoreType.DMA((2, 8)),
        ],
        compiler_params=params(SMALL),
        cost_estimate=pl.CostEstimate(flops=8_000_000_000, bytes_accessed=1000, transcendentals=0),
        name="weight_sums",
    )(scal, *pieces, ctx)


def ctx_grad_kernel(groups, cuts, scal, weight, *rest):
    pieces, rest = rest[: 5 * groups], rest[5 * groups :]
    out, gathered, (w, acc, low_acc, sems) = rest[0], rest[1 : 1 + groups], rest[1 + groups :]
    loads = []
    for g, (start, stop) in enumerate(cuts):
        sem = lambda n, g=g: sems.at[6 * g + n]
        cols = pltpu.make_async_copy(weight.at[:, start:stop], w.at[:, start:stop], sem(5))
        loads.append(gather_copies(scal[1], pieces[5 * g : 5 * g + 5], gathered[g], sem) + [cols])
        for c in loads[-1]:
            c.start()
    tiles, blocks, tokens, _ = gathered[0].shape
    rows = tiles * blocks * tokens
    step = rows // 3
    for g, (start, stop) in enumerate(cuts):
        for c in loads[g]:
            c.wait()
        for n in range(3):
            cot = gathered[g][n * (tiles // 3) : (n + 1) * (tiles // 3)].reshape(step, stop - start)
            part = lax.dot_general(cot, w[:, start:stop], NT, preferred_element_type=F32)
            at = slice(n * step, (n + 1) * step)
            part = part if g == 0 else acc[at, :] + part
            if g < groups - 1:
                acc[at, :] = part
            else:
                low_acc[at, :] = part.astype(BF16)
    store = pltpu.make_async_copy(low_acc, out, sems.at[6 * groups])
    store.start()
    store.wait()


def context_gradient(scal, weight, pieces, cuts):
    groups = len(cuts)
    tiles, tokens, _ = pieces[0][0].shape
    rows, width = weight.shape
    depth = tiles * 4 * tokens
    any_spec = pl.BlockSpec(memory_space=pl.ANY)
    return pl.pallas_call(
        functools.partial(ctx_grad_kernel, groups, cuts),
        in_specs=[pl.BlockSpec(memory_space=pltpu.SMEM)] + [any_spec] * (1 + 5 * groups),
        out_specs=any_spec,
        out_shape=jax.ShapeDtypeStruct((depth, rows), BF16),
        scratch_shapes=[pltpu.VMEM((tiles, 4, tokens, stop - start), BF16) for start, stop in cuts]
        + [
            pltpu.VMEM((rows, width), BF16),
            pltpu.VMEM((depth, rows), F32),
            pltpu.VMEM((depth, rows), BF16),
            pltpu.SemaphoreType.DMA((6 * groups + 1,)),
        ],
        compiler_params=params(LARGE),
        cost_estimate=pl.CostEstimate(flops=8_000_000_000, bytes_accessed=1000, transcendentals=0),
        name="context_gradient",
    )(scal, weight, *[p for some in pieces for p in some])


def backward_kernel(scal, ctx_grad, qkv, probs, out, ctx_grad_v, qkv_v, probs_v, out_v, grads, sems):
    tiles, heads, tokens, three = qkv_v.shape
    hd = three // 3
    factor = hd ** (-0.5)

    def loads(t):
        rows = pl.ds(pl.multiple_of(t * tokens, tokens), tokens)
        return [
            pltpu.make_async_copy(ctx_grad.at[rows], ctx_grad_v.at[rows], sems.at[0, t]),
            pltpu.make_async_copy(qkv.at[t], qkv_v.at[t], sems.at[1, t]),
            pltpu.make_async_copy(probs.at[t], probs_v.at[t], sems.at[2, t]),
        ]

    def store(t):
        return pltpu.make_async_copy(out_v.at[t], out.at[t], sems.at[3, t])

    for t in range(tiles):
        for c in loads(t):
            c.start()

    def one_tile(t, carry):
        for c in loads(t):
            c.wait()

        @pl.when(t < scal[0])
        def _():
            rows = pl.ds(pl.multiple_of(t * tokens, tokens), tokens)
            q, k, v = (qkv_v[t, :, :, n * hd : (n + 1) * hd] for n in range(3))
            dctx = [ctx_grad_v[rows, h * hd : (h + 1) * hd] for h in range(heads)]
            probs_wide = probs_v[t]
            low = probs_wide.astype(BF16)
            prob_grad = [lax.dot_general(v[h], dctx[h], NT, preferred_element_type=F32) for h in range(heads)]
            value_grad = [jnp.dot(low[h], dctx[h], preferred_element_type=F32) for h in range(heads)]
            prob_grad = jnp.stack(prob_grad)
            centre = jnp.sum(probs_wide * prob_grad, axis=1, keepdims=True)
            score_grad = (probs_wide * (prob_grad - centre) * factor).astype(BF16)
            key_grad = [jnp.dot(score_grad[h], q[h], preferred_element_type=F32) for h in range(heads)]
            query_grad = [
                lax.dot_general(score_grad[h], k[h], TN, preferred_element_type=F32) for h in range(heads)
            ]
            for h in range(heads):
                grads[h, :, 0:hd] = query_grad[h].astype(BF16)
                grads[h, :, hd : 2 * hd] = key_grad[h].astype(BF16)
                grads[h, :, 2 * hd : 3 * hd] = value_grad[h].astype(BF16)
            out_v[t] = jnp.swapaxes(grads[...], 0, 1)

        @pl.when(t >= scal[0])
        def _():
            out_v[t] = jnp.zeros(out_v.shape[1:], BF16)

        store(t).start()
        return carry

    lax.fori_loop(0, tiles, one_tile, 0)
    for t in range(tiles):
        store(t).wait()


def backward(scal, ctx_grad, qkv, probs):
    tiles, heads, tokens, three = qkv.shape
    any_spec = pl.BlockSpec(memory_space=pl.ANY)
    return pl.pallas_call(
        backward_kernel,
        in_specs=[pl.BlockSpec(memory_space=pltpu.SMEM)] + [any_spec] * 3,
        out_specs=any_spec,
        out_shape=jax.ShapeDtypeStruct((tiles, tokens, heads, three), BF16),
        scratch_shapes=[
            pltpu.VMEM(ctx_grad.shape, BF16),
            pltpu.VMEM(qkv.shape, BF16),
            pltpu.VMEM(probs.shape, F32),
            pltpu.VMEM((tiles, tokens, heads, three), BF16),
            pltpu.VMEM((heads, tokens, three), BF16),
            pltpu.SemaphoreType.DMA((4, tiles)),
        ],
        compiler_params=params(LARGE),
        cost_estimate=pl.CostEstimate(flops=8_000_000_000, bytes_accessed=1000, transcendentals=0),
        name="backward",
    )(scal, ctx_grad, qkv, probs)


def body(cuts, projections, cotangent, out_weight, tile_counts, fragment, drift):
    dp_size = lax.axis_size("dp")
    fsdp_size = lax.axis_size("fsdp")
    rep_size = lax.axis_size("rep")
    heads, hd, width = out_weight.shape
    me = lax.axis_index("dp")
    core = me % 2

    def flip_core():
        return [(i, i ^ 1) for i in range(dp_size)]

    def shift_x(s):
        return [(i, (i + s) % fsdp_size) for i in range(fsdp_size)]

    slots = [2 * k + (core ^ dc) for dc in range(2) for k in range(dp_size // 2)]
    same_core = [list(range(c, dp_size, 2)) for c in range(2)]
    scal = jnp.stack([tile_counts[0, me], lax.axis_index("fsdp"), *slots]).astype(jnp.int32)

    weight = out_weight.reshape(heads * hd, width)
    n = len(cuts)
    tiles = projections.shape[0]
    st = dict(cot=cotangent)

    def fence(*names):
        flat, tree = jax.tree.flatten({name: st[name] for name in names})
        st.update(jax.tree.unflatten(tree, lax.optimization_barrier(flat)))

    def send_own(i):
        start, stop = cuts[i]
        st[f"own{i}"] = st["cot"][:, :, start:stop]
        st[f"near{i}"] = (
            lax.ppermute(st[f"own{i}"], "fsdp", shift_x(-1)),
            lax.ppermute(st[f"own{i}"], "fsdp", shift_x(1)),
        )

    def pass_on(i):
        split = (tiles + i % 2) // 2
        plus1, minus1 = st[f"near{i}"]
        st[f"far{i}"] = (
            lax.ppermute(plus1[:split], "fsdp", shift_x(-1)),
            lax.ppermute(minus1[split:], "fsdp", shift_x(1)),
        )

    def pieces(i):
        plus1, minus1 = st[f"near{i}"]
        return (st[f"own{i}"], plus1, *st[f"far{i}"], minus1)

    def sum_chunk(i):
        st[f"keep{i}"], st[f"send{i}"] = weight_sums(scal, pieces(i), st["ctx"])

    def cross_core(i):
        st[f"core{i}"] = lax.ppermute(st[f"send{i}"], "dp", flip_core())

    send_own(0)
    send_own(1)
    qkv, probs, st["ctx"] = forward(scal, projections)
    frag_width = width // FRAGS
    picked = lax.dynamic_slice_in_dim(drift[0], fragment[0] * frag_width, frag_width, 2).astype(BF16)
    every = jnp.broadcast_to(picked[None], (rep_size, *picked.shape))
    st["drift"] = lax.all_to_all(every, "rep", 0, 0, tiled=True)
    fence("ctx", "drift", "near0", "cot")
    pass_on(0)
    send_own(2)
    fence("ctx", "near1", "far0")
    pass_on(1)
    sum_chunk(0)
    fence("near2", "keep0", "send0")
    pass_on(2)
    cross_core(0)
    fence("ctx", "far1")
    sum_chunk(1)
    fence("ctx", "far2", "keep0", "core0", "keep1", "send1")
    cross_core(1)
    sum_chunk(2)
    fence("keep0", "core0", "keep1", "core1", "keep2", "send2", "far2")
    cross_core(2)
    early = [(st[f"keep{i}"].astype(F32) + st[f"core{i}"].astype(F32)).astype(BF16) for i in (0, 1)]
    st["sums"] = jnp.concatenate(early + [jnp.zeros_like(st["keep2"])], axis=2)
    fence("sums", "keep2", "core2")
    late = (st["keep2"].astype(F32) + st["core2"].astype(F32)).astype(BF16)
    sums = lax.dynamic_update_slice(st["sums"], late, (0, 0, cuts[2][0]))
    summed = [lax.all_to_all(sums, "dp", 0, 0, axis_index_groups=same_core, tiled=True)]
    ctx_grad = context_gradient(scal, weight, [pieces(i) for i in range(n)], cuts)
    gradients = backward(scal, ctx_grad, qkv, probs)
    weight_grad = jnp.concatenate([jnp.sum(p.astype(F32), axis=0) for p in summed], axis=1) / (CAP * dp_size)
    synced = jnp.sum(st["drift"].astype(F32), axis=0) / rep_size
    return gradients, weight_grad.reshape(drift.shape), synced


def solution(mesh):
    sizes = [8, 10, 7]
    edges = [0]
    for size in sizes:
        edges.append(edges[-1] + size * LANES)
    cuts = list(zip(edges[:-1], edges[1:]))
    return jax.shard_map(
        functools.partial(body, cuts),
        mesh=mesh,
        in_specs=(
            P(("rep", "dp"), None, "fsdp", None),
            P(("rep", "dp"), "fsdp", None),
            P("fsdp", None, None),
            P("rep", None),
            P(),
            P("rep", "fsdp", "dp", None),
        ),
        out_specs=(
            P(("rep", "dp"), None, "fsdp", None),
            P("rep", "fsdp", "dp", None),
            P("fsdp", "dp", None),
        ),
        check_vma=False,
    )
```
